512 devices in a mesh: seq: 32 (over x_lo, y, core), head: 16 (over z, x_hi).
Axes of the slice: x: 4 (x_hi: 2, x_lo: 2; x = x_hi * 2 + x_lo), y: 8, z: 8, core: 2. Of those that a mesh axis runs over, the one named last changes fastest.
Arguments:
- queries: bfloat16 [32768, 4096], P(('seq', 'head')), may hold values from -200 to 200
- keys: bfloat16 [32768, 2048], P(('seq', 'head')), may hold values from -6.5 to 6.5
- values: bfloat16 [32768, 2048], P(('seq', 'head')), may hold values from -6 to 6
- visible: int32 [32, 4], P('seq'), may hold values 0 or 1
Outputs:
- attended: bfloat16 [32768, 4096], P(('seq', 'head'))
The draws below stay inside these ranges and needn't reach their ends.
All inputs are finite; a program needn't handle non-finite values. No bound on the sum of `visible` on one device may be relied on, other than what follows from the above.
Results may differ from the reference program's by a relative error of at most 0.0045.
Values may be sent and summed in bfloat16 or wider, within the bound.
A program may use at most 128 MiB of HBM per device.

```python
import jax
import jax.numpy as jnp
from jax import lax

HEAD_SIZE = 128
QUERY_PER_KV = 2
KEY_VALUE_HEADS = 16
HQ = 32
SEQUENCE_TOKENS = 32768
N_SEQ = 32


def joint_draw(key):
    query_key = jax.random.fold_in(key, 11)
    key_random_seed = jax.random.fold_in(key, 12)
    query_vals = jnp.clip(jax.random.normal(query_key, (SEQUENCE_TOKENS, HQ * HEAD_SIZE), jnp.float32), -6.0, 6.0)
    key_samples = jnp.clip(jax.random.normal(key_random_seed, (SEQUENCE_TOKENS, KEY_VALUE_HEADS * HEAD_SIZE), jnp.float32), -6.0, 6.0)
    return (query_vals, key_samples)


def draw_queries(key, part):
    return joint_draw(key)[0].astype(jnp.bfloat16)


def draw_keys(key, part):
    return joint_draw(key)[1].astype(jnp.bfloat16)


def place_ends(array, rng, low, largest):
    dims = array.shape
    index_at = [jax.random.randint(jax.random.fold_in(rng, axis), (), 0, dims[axis]) for axis in range(len(dims))]
    array = array.at[tuple(index_at)].set(low)
    longest = dims.index(max(dims))
    index_at[longest] = (index_at[longest] + 1) % dims[longest]
    return array.at[tuple(index_at)].set(largest)


def block_scale(stream_key, extent, pieces, low, largest):
    def one(position, parts):
        steps = jax.random.uniform(jax.random.fold_in(jax.random.fold_in(stream_key, 6), position), (parts,), jnp.float32, low / len(pieces), largest / len(pieces))
        return jnp.repeat(jnp.exp(steps), extent[position] // parts).reshape((-1,) + (1,) * (len(extent) - position - 1))

    factor_of = one(*pieces[0])
    for cut in pieces[1:]:
        factor_of = factor_of * one(*cut)
    return factor_of


def gaussian(own_key, dims, scale, reach, shards=(), kind=jnp.bfloat16):
    array = scale * jax.random.normal(own_key, dims, jnp.float32)
    if shards:
        array = array * block_scale(own_key, dims, shards, -0.22, 0.18)
    return jnp.clip(array, -reach, reach).astype(kind)


def setup_inputs(seed: int = 0) -> dict:
    seeds = jax.random.split(jax.random.key(seed), 5)
    return {
        "queries": draw_queries(jax.random.fold_in(seeds[4], 71), 0),
        "keys": draw_keys(jax.random.fold_in(seeds[4], 71), 0),
        "values": gaussian(seeds[2], (SEQUENCE_TOKENS, KEY_VALUE_HEADS * HEAD_SIZE), 1.0, 6.0, ((0, 512),)),
        "visible": place_ends((jax.random.randint(seeds[3], (N_SEQ, 4), 0, 4) < 3).astype(jnp.int32), jax.random.fold_in(seeds[3], 1), 0, 1),
    }


attn_scale = 168.0 ** -0.5
powers = (1, 2, 4, 8)


def reference(queries, keys, values, visible):
    tokens_all = queries.shape[0]
    block_length = tokens_all // N_SEQ
    query_block_list = queries.reshape(N_SEQ, block_length, KEY_VALUE_HEADS, QUERY_PER_KV, HEAD_SIZE)
    key_block_list = keys.reshape(N_SEQ, block_length, KEY_VALUE_HEADS, HEAD_SIZE)
    value_block_list = values.reshape(N_SEQ, block_length, KEY_VALUE_HEADS, HEAD_SIZE)

    def one_block(index):
        index = index.astype(jnp.int32)
        own_query = lax.dynamic_index_in_dim(query_block_list, index, 0, keepdims=False)
        key_list = [lax.dynamic_index_in_dim(key_block_list, index, 0, keepdims=False)]
        value_list = [lax.dynamic_index_in_dim(value_block_list, index, 0, keepdims=False)]
        flags = []
        for slot, distance in enumerate(powers):
            source = jnp.maximum(index - distance, 0).astype(jnp.int32)
            key_list.append(lax.dynamic_index_in_dim(key_block_list, source, 0, keepdims=False))
            value_list.append(lax.dynamic_index_in_dim(value_block_list, source, 0, keepdims=False))
            flags.append((visible[index, slot] != 0) & (index >= distance))
        all_keys = jnp.concatenate(key_list, axis=0)
        all_values = jnp.concatenate(value_list, axis=0)
        scores = jnp.einsum("qhgd,khd->hgqk", own_query.astype(jnp.float32), all_keys.astype(jnp.float32)) * attn_scale
        row_index = jnp.arange(block_length)[:, None]
        column = jnp.arange(5 * block_length)[None, :]
        region = column // block_length
        flag_arr = jnp.stack(flags)
        remote_ok = jnp.any((region[None] == (jnp.arange(4) + 1)[:, None, None]) & flag_arr[:, None, None], axis=0)
        allowed = jnp.where(region == 0, column <= row_index, remote_ok)
        masked = jnp.where(allowed, scores, -1e30)
        peak = jnp.max(masked, axis=-1, keepdims=True)
        weights = jnp.where(allowed, jnp.exp(masked - peak), 0.0)
        total = jnp.sum(weights, axis=-1)
        rounded = lax.optimization_barrier(weights.astype(jnp.bfloat16))
        numer = jnp.einsum("hgqk,khd->qhgd", rounded.astype(jnp.float32), all_values.astype(jnp.float32))
        return (numer / jnp.transpose(total, (2, 0, 1))[..., None]).astype(jnp.bfloat16)

    result = lax.map(one_block, jnp.arange(N_SEQ, dtype=jnp.int32))
    return result.reshape(tokens_all, HQ * HEAD_SIZE)
```

```python
import functools

import jax
import jax.numpy as jnp
from jax import lax
from jax.experimental import pallas as pl
from jax.experimental.pallas import tpu as pltpu
from jax.sharding import PartitionSpec as P

D = 128
RUN = 128
NZ = 8
BLOCK = 1024
SCALE2 = 168.0 ** (-0.5) * 1.4426950408889634
NM = 5
HIDE = 1e30
MESH = pl.DeviceIdType.MESH
F32 = jnp.float32
BF16 = jnp.bfloat16


def offset(i):
    return jnp.where(i % 2 == 1, (i + 1) // 2, (NZ - i // 2) % NZ)


def kernel(vis_ref, q_ref, k_ref, v_ref, o_ref, qbuf, kv, relay, vx, obuf, acc, peak,
           s_a, s_b, p_a, p_b,
           kv0_sem, q_sem, kv_sem, rl_sem, o_sem, in_send, f1_send, f2_send, f3_send, f4_send,
           m_send, mr_send, o_send):
    s = lax.axis_index("seq")
    h = lax.axis_index("head")
    z, xh = h // 2, h % 2
    core, chip = s % 2, s // 2
    xl, y = chip // 8, chip % 8
    relay_to = (xl * 8 + (y + 6) % 8) * 2 + core
    relay_chip = xl * 8 + (y + 2) % 8
    relay_from = relay_chip * 2 + core
    relays = relay_chip < 12
    relay_dst = relay_from + 8
    src8 = s - 8
    chip8 = src8 // 2
    relay_src = ((chip8 // 8) * 8 + (chip8 % 8 + 6) % 8) * 2 + core

    bar = pltpu.get_barrier_semaphore()

    @pl.loop(1, 16)
    def _(n):
        pl.semaphore_signal(bar, inc=1, device_id={"head": (h + n) % 16}, device_id_type=MESH)

    links = [
        (True, s + 1 - 2 * core),
        (s + 2 < 32, s + 2), (s >= 2, s - 2),
        (s + 4 < 32, s + 4), (s >= 4, s - 4),
        (s + 8 < 32, relay_to), (relays, relay_from),
        (relays, relay_dst), (s >= 8, relay_src),
    ]
    count = 15
    for cond, other in links:
        if cond is True:
            pl.semaphore_signal(bar, inc=1, device_id={"seq": other}, device_id_type=MESH)
            count = count + 1
        else:
            @pl.when(cond)
            def _():
                pl.semaphore_signal(bar, inc=1, device_id={"seq": other}, device_id_type=MESH)
            count = count + cond.astype(jnp.int32)
    pl.semaphore_wait(bar, count)

    def rows64(x):
        return pl.ds(pl.multiple_of(x * 64, 64), 64)

    def cols(i, width):
        return pl.ds(pl.multiple_of(i * width, width), width)

    def pieces(p):
        yield k_ref.at[:, cols(p, D)], kv.at[0, z, 0, rows64(xh)], in_send.at[0], kv0_sem.at[z]
        yield v_ref.at[:, cols(p, D)], kv.at[0, z, 1, rows64(xh)], in_send.at[1], kv0_sem.at[z]

    def q_pieces(p):
        for g in range(2):
            yield q_ref.at[:, cols(p * 2 + g, D)], qbuf.at[z, g, rows64(xh)], in_send.at[2], q_sem.at[z]

    for src, dst, _, sem in pieces(h):
        pltpu.make_async_copy(src, dst, sem).start()
    for src, dst, _, sem in q_pieces(h):
        pltpu.make_async_copy(src, dst, sem).start()
    for each in (pieces, q_pieces):
        @pl.loop(1, 16)
        def _(n):
            p = ((z + offset(n // 2)) % NZ) * 2 + (xh + n) % 2
            for src, dst, send, recv in each(p):
                pltpu.make_async_remote_copy(src, dst, send, recv, device_id={"head": p}, device_id_type=MESH).start()

    def zof(i):
        return (z + offset(i)) % NZ

    def wait_bytes(ref, sem):
        pltpu.make_async_copy(ref, ref, sem).wait()

    def pass_on(src, dst, send, recv, to):
        pltpu.make_async_remote_copy(src, dst, send, recv, device_id={"seq": to}, device_id_type=MESH).start()

    def own(i):
        r = zof(i)
        wait_bytes(kv.at[0, r], kv0_sem.at[r])

        @pl.when(core == 0)
        def _():
            pass_on(kv.at[0, r], kv.at[1, r], f1_send, kv_sem.at[0, r], s + 1)

        @pl.when(s + 2 < 32)
        def _():
            pass_on(kv.at[0, r], kv.at[2, r], f2_send, kv_sem.at[1, r], s + 2)

        @pl.when((s + 8 < 32) & (i < NM))
        def _():
            pass_on(kv.at[0, r], relay.at[i], m_send, rl_sem.at[i], relay_to)

    def two_back(i):
        r = zof(i)

        @pl.when(s >= 2)
        def _():
            wait_bytes(kv.at[2, r], kv_sem.at[1, r])

        @pl.when((s >= 2) & (core == 1))
        def _():
            pass_on(kv.at[2, r], kv.at[1, r], f1_send, kv_sem.at[0, r], s - 1)

    def to_four(i):
        r = zof(i)

        @pl.when((s >= 2) & (s + 2 < 32))
        def _():
            pass_on(kv.at[2, r], kv.at[3, r], f3_send, kv_sem.at[2, r], s + 2)

    def four_back(i):
        r = zof(i)

        @pl.when(s >= 4)
        def _():
            wait_bytes(kv.at[3, r], kv_sem.at[2, r])

        @pl.when((s >= 4) & (s + 4 < 32) & (i >= NM))
        def _():
            pass_on(kv.at[3, r], kv.at[4, r], f4_send, kv_sem.at[3, r], s + 4)

    def relayed(i):
        r = zof(i)

        @pl.when(relays)
        def _():
            wait_bytes(relay.at[i], rl_sem.at[i])
            pass_on(relay.at[i], kv.at[4, r], mr_send, kv_sem.at[3, r], relay_dst)

    for j, dist in ((1, 1), (2, 2), (3, 4), (4, 8)):
        @pl.when(s < dist)
        def _():
            kv[j] = jnp.zeros(kv.shape[1:], BF16)
    for j in range(5):
        vx[j, :, D:] = jnp.ones((BLOCK, D), BF16)

    for k in range(NZ):
        own(k)
        if k >= 2:
            two_back(k - 2)
        if k in (3, 5, 7):
            relayed((k - 3) // 2)
    two_back(6)
    two_back(7)

    @pl.loop(0, NZ)
    def _(i):
        to_four(i)

    @pl.when(s >= 1)
    def _():
        @pl.loop(0, NZ)
        def _(i):
            wait_bytes(kv.at[1, i], kv_sem.at[0, i])

    for j in range(3):
        vx[j, :, :D] = kv[j, :, 1].reshape(BLOCK, D)

    flags = [(vis_ref[0, j] != 0) & (s >= 2 ** j) for j in range(4)]
    dims = (((1,), (1,)), ((), ()))

    def scores3(i, buf):
        r = zof(i)
        wait_bytes(qbuf.at[r], q_sem.at[r])
        q = qbuf[r].reshape(2 * RUN, D)
        for j in range(3):
            buf[:, j * BLOCK:(j + 1) * BLOCK] = lax.dot_general(
                q, kv[j, :, 0].reshape(BLOCK, D), dims, preferred_element_type=F32)

    row = lax.broadcasted_iota(jnp.int32, (2 * RUN, BLOCK), 0) % RUN
    column = lax.broadcasted_iota(jnp.int32, (2 * RUN, BLOCK), 1)
    ahead = column - row

    def soft3(i, buf, out):
        r = zof(i)
        s0 = jnp.where(ahead <= r * RUN, buf[:, :BLOCK], -HIDE)
        s1, s2 = buf[:, BLOCK:2 * BLOCK], buf[:, 2 * BLOCK:]
        top = jnp.max(s0, axis=1, keepdims=True)
        for part, flag in ((s1, flags[0]), (s2, flags[1])):
            here = jnp.max(part, axis=1, keepdims=True)
            top = jnp.where(flag, jnp.maximum(top, here), top)
        low = top * SCALE2
        peak[r] = jnp.broadcast_to(low, (2 * RUN, D))
        out[:, :BLOCK] = jnp.exp2(s0 * SCALE2 - low).astype(BF16)
        for n, (part, flag) in enumerate(((s1, flags[0]), (s2, flags[1]))):
            out[:, (n + 1) * BLOCK:(n + 2) * BLOCK] = jnp.exp2(
                part * SCALE2 - jnp.where(flag, low, HIDE)).astype(BF16)

    def value3(i, out):
        acc[zof(i)] = jnp.dot(out[...], vx[0:3].reshape(3 * BLOCK, 2 * D), preferred_element_type=F32)

    scores3(0, s_a)
    scores3(1, s_b)
    soft3(0, s_a, p_a)

    @pl.loop(0, 3)
    def _(n):
        i = 2 * n

        relayed_if(relayed, n + 3)
        value3(i, p_a)
        scores3(i + 2, s_a)
        soft3(i + 1, s_b, p_b)
        value3(i + 1, p_b)
        scores3(i + 3, s_b)
        soft3(i + 2, s_a, p_a)

    value3(6, p_a)
    soft3(7, s_b, p_b)
    value3(7, p_b)

    @pl.loop(0, NZ)
    def _(i):
        four_back(i)

    def scores1(j, i, buf):
        buf[:, :BLOCK] = lax.dot_general(
            qbuf[zof(i)].reshape(2 * RUN, D), kv[j, :, 0].reshape(BLOCK, D), dims, preferred_element_type=F32)

    def soft1(j, i, buf, out):
        r = zof(i)
        flag = flags[j - 1]
        part = buf[:, :BLOCK]
        old = peak[r, :, 0:1]
        low = jnp.where(flag, jnp.maximum(old, jnp.max(part, axis=1, keepdims=True) * SCALE2), old)
        peak[r] = jnp.broadcast_to(low, (2 * RUN, D))
        acc[r] = acc[r] * jnp.exp2(old - low)
        out[:, :BLOCK] = jnp.exp2(part * SCALE2 - jnp.where(flag, low, HIDE)).astype(BF16)

    def value1(j, i, out):
        r = zof(i)
        total = acc[r] + jnp.dot(out[:, :BLOCK], vx[j], preferred_element_type=F32)
        if j < 4:
            acc[r] = total
            return
        done = (total[:, :D] / total[:, D:]).astype(BF16)
        obuf[r, :, :D] = done[:RUN]
        obuf[r, :, D:] = done[RUN:]
        for x in range(2):
            p = r * 2 + x
            src, dst = obuf.at[r, x * 64:(x + 1) * 64], o_ref.at[:, cols(h, 2 * D)]

            @pl.when(p == h)
            def _():
                pltpu.make_async_copy(src, dst, o_sem).start()

            @pl.when(p != h)
            def _():
                pltpu.make_async_remote_copy(src, dst, o_send, o_sem, device_id={"head": p}, device_id_type=MESH).start()

    def block(j):
        vx[j, :, :D] = kv[j, :, 1].reshape(BLOCK, D)
        scores1(j, 7, s_a)
        scores1(j, 6, s_b)
        soft1(j, 7, s_a, p_a)

        @pl.loop(0, 3)
        def _(n):
            i = 7 - 2 * n
            value1(j, i, p_a)
            scores1(j, i - 2, s_a)
            soft1(j, i - 1, s_b, p_b)
            value1(j, i - 1, p_b)
            scores1(j, i - 3, s_b)
            soft1(j, i - 2, s_a, p_a)

        value1(j, 1, p_a)
        soft1(j, 0, s_b, p_b)
        value1(j, 0, p_b)

    block(3)

    @pl.when(s >= 8)
    def _():
        @pl.loop(0, NZ)
        def _(i):
            wait_bytes(kv.at[4, i], kv_sem.at[3, i])

    block(4)

    wait_bytes(k_ref.at[:, :15 * D], in_send.at[0])
    wait_bytes(v_ref.at[:, :15 * D], in_send.at[1])
    wait_bytes(q_ref.at[:, :30 * D], in_send.at[2])
    whole = kv.at[0]
    for cond, ref, sem in (
        ((core == 0) | (s >= 2), whole, f1_send),
        (s + 2 < 32, whole, f2_send),
        ((s >= 2) & (s + 2 < 32), whole, f3_send),
        ((s >= 4) & (s + 4 < 32), kv.at[0, 0:NZ - NM], f4_send),
        (s + 8 < 32, kv.at[0, 0:NM], m_send),
        (relays, kv.at[0, 0:NM], mr_send),
    ):
        @pl.when(cond)
        def _():
            wait_bytes(ref, sem)
    wait_bytes(o_ref.at[:, :30 * D], o_send)
    wait_bytes(o_ref, o_sem)


def relayed_if(relayed, i):
    @pl.when(i < NM)
    def _():
        relayed(i)


def body(queries, keys, values, visible):
    dma = pltpu.SemaphoreType.DMA
    return pl.pallas_call(
        kernel,
        out_shape=jax.ShapeDtypeStruct(queries.shape, BF16),
        in_specs=[pl.BlockSpec(memory_space=pltpu.SMEM)] + [pl.BlockSpec(memory_space=pl.ANY)] * 3,
        out_specs=pl.BlockSpec(memory_space=pl.ANY),
        scratch_shapes=[
            pltpu.VMEM((NZ, 2, RUN, D), BF16),
            pltpu.VMEM((5, NZ, 2, RUN, D), BF16),
            pltpu.VMEM((NM, 2, RUN, D), BF16),
            pltpu.VMEM((5, BLOCK, 2 * D), BF16),
            pltpu.VMEM((NZ, RUN, 2 * D), BF16),
            pltpu.VMEM((NZ, 2 * RUN, 2 * D), F32),
            pltpu.VMEM((NZ, 2 * RUN, D), F32),
            pltpu.VMEM((2 * RUN, 3 * BLOCK), F32),
            pltpu.VMEM((2 * RUN, 3 * BLOCK), F32),
            pltpu.VMEM((2 * RUN, 3 * BLOCK), BF16),
            pltpu.VMEM((2 * RUN, 3 * BLOCK), BF16),
            dma((NZ,)), dma((NZ,)), dma((4, NZ)), dma((NM,)), dma,
            dma((3,)), dma, dma, dma, dma, dma, dma, dma,
        ],
        compiler_params=pltpu.CompilerParams(
            collective_id=0, has_side_effects=True, vmem_limit_bytes=56 * 2**20),
        cost_estimate=pl.CostEstimate(flops=5 * 10**9, bytes_accessed=2 * 10**6, transcendentals=10**7),
    )(visible, queries, keys, values)


def solution(mesh):
    rows = P(("seq", "head"), None)
    return jax.shard_map(
        body,
        mesh=mesh,
        in_specs=(rows, rows, rows, P("seq", None)),
        out_specs=rows,
        check_vma=False,
    )
```

```python
import functools

import jax
import jax.numpy as jnp
from jax import lax
from jax.experimental import pallas as pl
from jax.experimental.pallas import tpu as pltpu
from jax.sharding import PartitionSpec as P

D = 128
RUN = 128
NZ = 8
BLOCK = 1024
SCALE2 = 168.0 ** (-0.5) * 1.4426950408889634
AHEAD = 8
NM = 5
HIDE = 1e30
PLAN = (
    ("own", 0),
    ("own", 1),
    ("own", 2),
    ("two", 0),
    ("four", 0),
    ("relay", 0),
    ("own", 3),
    ("own", 4),
    ("two", 1),
    ("four", 1),
    ("two", 2),
    ("four", 2),
    ("relay", 1),
    ("own", 5),
    ("two", 3),
    ("four", 3),
    ("own", 6),
    ("two", 4),
    ("four", 4),
    ("own", 7),
    ("two", 5),
    ("four", 5),
    ("relay", 2),
    ("two", 6),
    ("four", 6),
    ("two", 7),
    ("four", 7),
)
LATER = (
    (("cross", 0),),
    (("cross", 1), ("relay", 3)),
    (("cross", 2), ("cross", 3)),
    (("cross", 4), ("relay", 4)),
    (("cross", 5), ("old", 0), ("old", 1), ("old", 2), ("old", 3), ("old", 4), ("old", 5)),
    (("cross", 6), ("old", 6)),
    (("cross", 7), ("old", 7)),
)
MESH = pl.DeviceIdType.MESH
F32 = jnp.float32
BF16 = jnp.bfloat16


def offset(i):
    return jnp.where(i % 2 == 1, (i + 1) // 2, (NZ - i // 2) % NZ)


def kernel(vis_ref, q_ref, k_ref, v_ref, o_ref, qbuf, kv, relay, cross, vx, obuf, acc, peak,
           s_a, s_b, p_a, p_b,
           kv0_sem, q_sem, kv_sem, rl_sem, cross_sem, o_sem, in_send, f1_send, f2_send, f3_send, f4_send,
           m_send, mr_send, cross_send, o_send):
    s = lax.axis_index("seq")
    h = lax.axis_index("head")
    z, xh = h // 2, h % 2
    core, chip = s % 2, s // 2
    xl, y = chip // 8, chip % 8

    def relay_of(c):
        return jnp.where((c >= 4) & (c < 8), c + 6, (c // 8) * 8 + (c % 8 + 6) % 8)

    relay_to = relay_of(chip) * 2 + core
    relays = (xl == 1) | (y >= 6) | (y <= 1)
    relay_from = jnp.where((y >= 2) & (y <= 5), y + 2, xl * 8 + (y + 2) % 8) * 2 + core
    relay_dst = relay_from + 8
    relay_src = relay_of(chip - 4) * 2 + core
    sends_cross, is_cross, gets_cross = chip == 7, chip == 15, chip == 8

    bar = pltpu.get_barrier_semaphore()

    @pl.loop(1, 16)
    def _(n):
        pl.semaphore_signal(bar, inc=1, device_id={"head": (h + n) % 16}, device_id_type=MESH)

    links = [
        (True, s + 1 - 2 * core),
        (s + 2 < 32, s + 2), (s >= 2, s - 2),
        (s + 4 < 32, s + 4), (s >= 4, s - 4),
        (s + 8 < 32, relay_to), (relays, relay_from),
        (relays, relay_dst), (s >= 8, relay_src),
        (sends_cross, 30 + core), (is_cross, 14 + core), (is_cross, 16 + core), (gets_cross, 30 + core),
    ]
    count = 15
    for cond, other in links:
        if cond is True:
            pl.semaphore_signal(bar, inc=1, device_id={"seq": other}, device_id_type=MESH)
            count = count + 1
        else:
            @pl.when(cond)
            def _():
                pl.semaphore_signal(bar, inc=1, device_id={"seq": other}, device_id_type=MESH)
            count = count + cond.astype(jnp.int32)
    pl.semaphore_wait(bar, count)

    def rows64(x):
        return pl.ds(pl.multiple_of(x * 64, 64), 64)

    def cols(i, width):
        return pl.ds(pl.multiple_of(i * width, width), width)

    def pieces(p):
        yield k_ref.at[:, cols(p, D)], kv.at[0, z, 0, rows64(xh)], in_send.at[0], kv0_sem.at[z]
        yield v_ref.at[:, cols(p, D)], kv.at[0, z, 1, rows64(xh)], in_send.at[1], kv0_sem.at[z]

    def q_pieces(p):
        for g in range(2):
            yield q_ref.at[:, cols(p * 2 + g, D)], qbuf.at[z, g, rows64(xh)], in_send.at[2], q_sem.at[z]

    for src, dst, _, sem in pieces(h):
        pltpu.make_async_copy(src, dst, sem).start()
    for src, dst, _, sem in q_pieces(h):
        pltpu.make_async_copy(src, dst, sem).start()

    def spread(i, each):
        for n in range(2):
            p = ((z + offset(i)) % NZ) * 2 + (xh + n) % 2

            @pl.when(p != h)
            def _():
                for src, dst, send, recv in each(p):
                    pltpu.make_async_remote_copy(
                        src, dst, send, recv, device_id={"head": p}, device_id_type=MESH).start()

    for i in range(AHEAD):
        spread(i, pieces)

    def zof(i):
        return (z + offset(i)) % NZ

    def wait_bytes(ref, sem):
        pltpu.make_async_copy(ref, ref, sem).wait()

    def pass_on(src, dst, send, recv, to):
        pltpu.make_async_remote_copy(src, dst, send, recv, device_id={"seq": to}, device_id_type=MESH).start()

    def own(i):
        r = zof(i)
        wait_bytes(kv.at[0, r], kv0_sem.at[r])
        if i + AHEAD < NZ:
            spread(i + AHEAD, pieces)
        else:
            spread(i + AHEAD - NZ, q_pieces)

        @pl.when(core == 0)
        def _():
            pass_on(kv.at[0, r], kv.at[1, r], f1_send, kv_sem.at[0, r], s + 1)

        @pl.when(s + 2 < 32)
        def _():
            pass_on(kv.at[0, r], kv.at[2, r], f2_send, kv_sem.at[1, r], s + 2)

        @pl.when((s + 8 < 32) & (i < NM))
        def _():
            pass_on(kv.at[0, r], relay.at[i], m_send, rl_sem.at[i], relay_to)

    def two_back(i):
        r = zof(i)

        @pl.when(s >= 2)
        def _():
            wait_bytes(kv.at[2, r], kv_sem.at[1, r])

        @pl.when((s >= 2) & (core == 1))
        def _():
            pass_on(kv.at[2, r], kv.at[1, r], f1_send, kv_sem.at[0, r], s - 1)

    def to_four(i):
        r = zof(i)

        @pl.when((s >= 2) & (s + 2 < 32) & (chip != 7))
        def _():
            pass_on(kv.at[2, r], kv.at[3, r], f3_send, kv_sem.at[2, r], s + 2)

        @pl.when(sends_cross)
        def _():
            pass_on(kv.at[2, r], cross.at[r], f3_send, cross_sem.at[r], 30 + core)

    def crossed(i):
        r = zof(i)

        @pl.when(is_cross)
        def _():
            wait_bytes(cross.at[r], cross_sem.at[r])
            pass_on(cross.at[r], kv.at[3, r], cross_send, kv_sem.at[2, r], 16 + core)

    def four_back(i):
        r = zof(i)

        @pl.when(s >= 4)
        def _():
            wait_bytes(kv.at[3, r], kv_sem.at[2, r])

        @pl.when((s >= 4) & (s + 4 < 32) & (i >= NM))
        def _():
            pass_on(kv.at[3, r], kv.at[4, r], f4_send, kv_sem.at[3, r], s + 4)

    def relayed(i):
        r = zof(i)

        @pl.when(relays)
        def _():
            wait_bytes(relay.at[i], rl_sem.at[i])
            pass_on(relay.at[i], kv.at[4, r], mr_send, kv_sem.at[3, r], relay_dst)

    for j, dist in ((1, 1), (2, 2), (3, 4), (4, 8)):
        @pl.when(s < dist)
        def _():
            kv[j] = jnp.zeros(kv.shape[1:], BF16)
    for j in range(5):
        vx[j, :, D:] = jnp.ones((BLOCK, D), BF16)

    for step, i in PLAN:
        if step == "own":
            own(i)
        elif step == "two":
            two_back(i)
        elif step == "four":
            to_four(i)
        elif step == "relay":
            relayed(i)
        else:
            crossed(i)

    @pl.when(s >= 1)
    def _():
        @pl.loop(0, NZ)
        def _(i):
            wait_bytes(kv.at[1, i], kv_sem.at[0, i])

    for j in range(3):
        vx[j, :, :D] = kv[j, :, 1].reshape(BLOCK, D)

    flags = [(vis_ref[0, j] != 0) & (s >= 2 ** j) for j in range(4)]
    dims = (((1,), (1,)), ((), ()))

    def scores3(i, buf):
        q = qbuf[zof(i)].reshape(2 * RUN, D)
        for j in range(3):
            buf[:, j * BLOCK:(j + 1) * BLOCK] = lax.dot_general(
                q, kv[j, :, 0].reshape(BLOCK, D), dims, preferred_element_type=F32)

    row = lax.broadcasted_iota(jnp.int32, (2 * RUN, BLOCK), 0) % RUN
    column = lax.broadcasted_iota(jnp.int32, (2 * RUN, BLOCK), 1)
    ahead = column - row

    def soft3(i, buf, out):
        r = zof(i)
        s0 = jnp.where(ahead <= r * RUN, buf[:, :BLOCK], -HIDE)
        s1, s2 = buf[:, BLOCK:2 * BLOCK], buf[:, 2 * BLOCK:]
        top = jnp.max(s0, axis=1, keepdims=True)
        for part, flag in ((s1, flags[0]), (s2, flags[1])):
            here = jnp.max(part, axis=1, keepdims=True)
            top = jnp.where(flag, jnp.maximum(top, here), top)
        low = top * SCALE2
        peak[r] = jnp.broadcast_to(low, (2 * RUN, D))
        out[:, :BLOCK] = jnp.exp2(s0 * SCALE2 - low).astype(BF16)
        for n, (part, flag) in enumerate(((s1, flags[0]), (s2, flags[1]))):
            out[:, (n + 1) * BLOCK:(n + 2) * BLOCK] = jnp.exp2(
                part * SCALE2 - jnp.where(flag, low, HIDE)).astype(BF16)

    def value3(i, out):
        acc[zof(i)] = jnp.dot(out[...], vx[0:3].reshape(3 * BLOCK, 2 * D), preferred_element_type=F32)

    def query(i):
        r = zof(i)
        wait_bytes(qbuf.at[r], q_sem.at[r])

        @pl.when(i + AHEAD < NZ)
        def _():
            spread(i + AHEAD, q_pieces)

    def events(at):
        for step, k in LATER[at]:
            {"relay": relayed, "cross": crossed, "old": four_back}[step](k)

    query(0)
    scores3(0, s_a)
    query(1)
    scores3(1, s_b)
    soft3(0, s_a, p_a)

    @pl.loop(0, 3)
    def _(n):
        i = 2 * n
        for at in range(3):
            @pl.when(n == at)
            def _():
                events(2 * at)
        query(i + 2)
        value3(i, p_a)
        scores3(i + 2, s_a)
        soft3(i + 1, s_b, p_b)
        for at in range(3):
            @pl.when(n == at)
            def _():
                events(2 * at + 1)
        query(i + 3)
        value3(i + 1, p_b)
        scores3(i + 3, s_b)
        soft3(i + 2, s_a, p_a)

    value3(6, p_a)
    soft3(7, s_b, p_b)
    value3(7, p_b)
    events(6)
    def scores1(j, i, buf):
        buf[:, :BLOCK] = lax.dot_general(
            qbuf[zof(i)].reshape(2 * RUN, D), kv[j, :, 0].reshape(BLOCK, D), dims, preferred_element_type=F32)

    def soft1(j, i, buf, out):
        r = zof(i)
        flag = flags[j - 1]
        part = buf[:, :BLOCK]
        old = peak[r, :, 0:1]
        low = jnp.where(flag, jnp.maximum(old, jnp.max(part, axis=1, keepdims=True) * SCALE2), old)
        peak[r] = jnp.broadcast_to(low, (2 * RUN, D))
        acc[r] = acc[r] * jnp.exp2(old - low)
        out[:, :BLOCK] = jnp.exp2(part * SCALE2 - jnp.where(flag, low, HIDE)).astype(BF16)

    def value1(j, i, out):
        r = zof(i)
        total = acc[r] + jnp.dot(out[:, :BLOCK], vx[j], preferred_element_type=F32)
        if j < 4:
            acc[r] = total
            return
        done = (total[:, :D] / total[:, D:]).astype(BF16)
        obuf[r, :, :D] = done[:RUN]
        obuf[r, :, D:] = done[RUN:]
        for x in range(2):
            p = r * 2 + x
            src, dst = obuf.at[r, x * 64:(x + 1) * 64], o_ref.at[:, cols(h, 2 * D)]

            @pl.when(p == h)
            def _():
                pltpu.make_async_copy(src, dst, o_sem).start()

            @pl.when(p != h)
            def _():
                pltpu.make_async_remote_copy(src, dst, o_send, o_sem, device_id={"head": p}, device_id_type=MESH).start()

    def block(j):
        vx[j, :, :D] = kv[j, :, 1].reshape(BLOCK, D)
        scores1(j, 7, s_a)
        scores1(j, 6, s_b)
        soft1(j, 7, s_a, p_a)

        @pl.loop(0, 3)
        def _(n):
            i = 7 - 2 * n
            value1(j, i, p_a)
            scores1(j, i - 2, s_a)
            soft1(j, i - 1, s_b, p_b)
            value1(j, i - 1, p_b)
            scores1(j, i - 3, s_b)
            soft1(j, i - 2, s_a, p_a)

        value1(j, 1, p_a)
        soft1(j, 0, s_b, p_b)
        value1(j, 0, p_b)

    block(3)

    @pl.when(s >= 8)
    def _():
        @pl.loop(0, NZ)
        def _(i):
            wait_bytes(kv.at[4, i], kv_sem.at[3, i])

    block(4)

    wait_bytes(k_ref.at[:, :15 * D], in_send.at[0])
    wait_bytes(v_ref.at[:, :15 * D], in_send.at[1])
    wait_bytes(q_ref.at[:, :30 * D], in_send.at[2])
    whole = kv.at[0]
    for cond, ref, sem in (
        ((core == 0) | (s >= 2), whole, f1_send),
        (s + 2 < 32, whole, f2_send),
        ((s >= 2) & (s + 2 < 32), whole, f3_send),
        ((s >= 4) & (s + 4 < 32), kv.at[0, 0:NZ - NM], f4_send),
        (s + 8 < 32, kv.at[0, 0:NM], m_send),
        (relays, kv.at[0, 0:NM], mr_send),
        (is_cross, whole, cross_send),
    ):
        @pl.when(cond)
        def _():
            wait_bytes(ref, sem)
    wait_bytes(o_ref.at[:, :30 * D], o_send)
    wait_bytes(o_ref, o_sem)


def body(queries, keys, values, visible):
    dma = pltpu.SemaphoreType.DMA
    return pl.pallas_call(
        kernel,
        out_shape=pltpu.VMEM(queries.shape, BF16),
        in_specs=[pl.BlockSpec(memory_space=pltpu.SMEM)] + [pl.BlockSpec(memory_space=pl.ANY)] * 3,
        out_specs=pl.BlockSpec(memory_space=pltpu.VMEM),
        scratch_shapes=[
            pltpu.VMEM((NZ, 2, RUN, D), BF16),
            pltpu.VMEM((5, NZ, 2, RUN, D), BF16),
            pltpu.VMEM((NM, 2, RUN, D), BF16),
            pltpu.VMEM((NZ, 2, RUN, D), BF16),
            pltpu.VMEM((5, BLOCK, 2 * D), BF16),
            pltpu.VMEM((NZ, RUN, 2 * D), BF16),
            pltpu.VMEM((NZ, 2 * RUN, 2 * D), F32),
            pltpu.VMEM((NZ, 2 * RUN, D), F32),
            pltpu.VMEM((2 * RUN, 3 * BLOCK), F32),
            pltpu.VMEM((2 * RUN, 3 * BLOCK), F32),
            pltpu.VMEM((2 * RUN, 3 * BLOCK), BF16),
            pltpu.VMEM((2 * RUN, 3 * BLOCK), BF16),
            dma((NZ,)), dma((NZ,)), dma((4, NZ)), dma((NM,)), dma((NZ,)), dma,
            dma((3,)), dma, dma, dma, dma, dma, dma, dma, dma,
        ],
        compiler_params=pltpu.CompilerParams(
            collective_id=0, has_side_effects=True, vmem_limit_bytes=56 * 2**20),
        cost_estimate=pl.CostEstimate(flops=5 * 10**9, bytes_accessed=2 * 10**6, transcendentals=10**7),
    )(visible, queries, keys, values)


def solution(mesh):
    rows = P(("seq", "head"), None)
    return jax.shard_map(
        body,
        mesh=mesh,
        in_specs=(rows, rows, rows, P("seq", None)),
        out_specs=rows,
        check_vma=False,
    )
```

```python
import functools

import jax
import jax.numpy as jnp
from jax import lax
from jax.experimental import pallas as pl
from jax.experimental.pallas import tpu as pltpu
from jax.sharding import PartitionSpec as P

D = 128
RUN = 128
NZ = 8
BLOCK = 1024
SCALE2 = 168.0 ** (-0.5) * 1.4426950408889634
AHEAD = 8
DOWN = (0, 1, 5, 6, 7)
NM = len(DOWN)
HIDE = 1e30
PLAN = (
    ("own", 0),
    ("own", 1),
    ("own", 2),
    ("two", 0),
    ("relay", 0),
    ("own", 3),
    ("own", 4),
    ("two", 1),
    ("relay", 1),
    ("two", 2),
    ("own", 5),
    ("two", 3),
    ("own", 6),
    ("two", 4),
    ("own", 7),
    ("four", 0),
    ("four", 1),
    ("four", 2),
    ("four", 3),
    ("four", 4),
    ("two", 5),
    ("four", 5),
    ("two", 6),
    ("four", 6),
    ("relay", 5),
    ("two", 7),
    ("four", 7),
)
LATER = (
    (("cross", 0), ("old", 0), ),
    (("cross", 1), ("old", 1), ("relay", 6), ),
    (("cross", 2), ("old", 2), ),
    (("cross", 3), ("old", 3), ("relay", 7), ),
    (("cross", 4), ("old", 4), ),
    (("cross", 5), ("old", 5), ),
    (("cross", 6), ("old", 6), ("cross", 7), ("old", 7), ),
)
MESH = pl.DeviceIdType.MESH
F32 = jnp.float32
BF16 = jnp.bfloat16


def offset(i):
    return jnp.where(i % 2 == 1, (i + 1) // 2, (NZ - i // 2) % NZ)


def kernel(vis_ref, q_ref, k_ref, v_ref, o_ref, qbuf, kv, relay, cross, vx, obuf, acc, peak,
           s_a, s_b, p_a, p_b,
           kv0_sem, q_sem, kv_sem, rl_sem, cross_sem, o_sem, in_send, f1_send, f2_send, f3_send, f4_send,
           m_send, mr_send, cross_send, o_send):
    s = lax.axis_index("seq")
    h = lax.axis_index("head")
    z, xh = h // 2, h % 2
    core, chip = s % 2, s // 2
    xl, y = chip // 8, chip % 8

    def relay_of(c):
        return jnp.where((c >= 4) & (c < 8), c + 6, (c // 8) * 8 + (c % 8 + 6) % 8)

    relay_to = relay_of(chip) * 2 + core
    relays = (xl == 1) | (y >= 6) | (y <= 1)
    relay_from = jnp.where((y >= 2) & (y <= 5), y + 2, xl * 8 + (y + 2) % 8) * 2 + core
    relay_dst = relay_from + 8
    relay_src = relay_of(chip - 4) * 2 + core
    sends_cross, is_cross, gets_cross = chip == 7, chip == 15, chip == 8

    bar = pltpu.get_barrier_semaphore()

    @pl.loop(1, 16)
    def _(n):
        pl.semaphore_signal(bar, inc=1, device_id={"head": (h + n) % 16}, device_id_type=MESH)

    links = [
        (True, s + 1 - 2 * core),
        (s + 2 < 32, s + 2), (s >= 2, s - 2),
        (s + 4 < 32, s + 4), (s >= 4, s - 4),
        (s + 8 < 32, relay_to), (relays, relay_from),
        (relays, relay_dst), (s >= 8, relay_src),
        (sends_cross, 30 + core), (is_cross, 14 + core), (is_cross, 16 + core), (gets_cross, 30 + core),
    ]
    count = 15
    for cond, other in links:
        if cond is True:
            pl.semaphore_signal(bar, inc=1, device_id={"seq": other}, device_id_type=MESH)
            count = count + 1
        else:
            @pl.when(cond)
            def _():
                pl.semaphore_signal(bar, inc=1, device_id={"seq": other}, device_id_type=MESH)
            count = count + cond.astype(jnp.int32)
    pl.semaphore_wait(bar, count)

    def rows64(x):
        return pl.ds(pl.multiple_of(x * 64, 64), 64)

    def cols(i, width):
        return pl.ds(pl.multiple_of(i * width, width), width)

    def pieces(p):
        yield k_ref.at[:, cols(p, D)], kv.at[0, z, 0, rows64(xh)], in_send.at[0], kv0_sem.at[z]
        yield v_ref.at[:, cols(p, D)], kv.at[0, z, 1, rows64(xh)], in_send.at[1], kv0_sem.at[z]

    def q_pieces(p):
        for g in range(2):
            yield q_ref.at[:, cols(p * 2 + g, D)], qbuf.at[z, g, rows64(xh)], in_send.at[2], q_sem.at[z]

    for src, dst, _, sem in pieces(h):
        pltpu.make_async_copy(src, dst, sem).start()
    for src, dst, _, sem in q_pieces(h):
        pltpu.make_async_copy(src, dst, sem).start()

    def spread(i, each):
        for n in range(2):
            p = ((z + offset(i)) % NZ) * 2 + (xh + n) % 2

            @pl.when(p != h)
            def _():
                for src, dst, send, recv in each(p):
                    pltpu.make_async_remote_copy(
                        src, dst, send, recv, device_id={"head": p}, device_id_type=MESH).start()

    for i in range(AHEAD):
        spread(i, pieces)

    def zof(i):
        return (z + offset(i)) % NZ

    def wait_bytes(ref, sem):
        pltpu.make_async_copy(ref, ref, sem).wait()

    def pass_on(src, dst, send, recv, to):
        pltpu.make_async_remote_copy(src, dst, send, recv, device_id={"seq": to}, device_id_type=MESH).start()

    def own(i):
        r = zof(i)
        wait_bytes(kv.at[0, r], kv0_sem.at[r])
        if i + AHEAD < NZ:
            spread(i + AHEAD, pieces)
        else:
            spread(i + AHEAD - NZ, q_pieces)

        @pl.when(core == 0)
        def _():
            pass_on(kv.at[0, r], kv.at[1, r], f1_send, kv_sem.at[0, r], s + 1)

        @pl.when(s + 2 < 32)
        def _():
            pass_on(kv.at[0, r], kv.at[2, r], f2_send, kv_sem.at[1, r], s + 2)

        if i in DOWN:
            n = DOWN.index(i)

            @pl.when(s + 8 < 32)
            def _():
                pass_on(kv.at[0, r], relay.at[n], m_send, rl_sem.at[n], relay_to)

    def two_back(i):
        r = zof(i)

        @pl.when(s >= 2)
        def _():
            wait_bytes(kv.at[2, r], kv_sem.at[1, r])

        @pl.when((s >= 2) & (core == 1))
        def _():
            pass_on(kv.at[2, r], kv.at[1, r], f1_send, kv_sem.at[0, r], s - 1)

    def to_four(i):
        r = zof(i)

        @pl.when((s >= 2) & (s + 2 < 32) & (chip != 7))
        def _():
            pass_on(kv.at[2, r], kv.at[3, r], f3_send, kv_sem.at[2, r], s + 2)

        @pl.when(sends_cross)
        def _():
            pass_on(kv.at[2, r], cross.at[r], f3_send, cross_sem.at[r], 30 + core)

    def crossed(i):
        r = zof(i)

        @pl.when(is_cross)
        def _():
            wait_bytes(cross.at[r], cross_sem.at[r])
            pass_on(cross.at[r], kv.at[3, r], cross_send, kv_sem.at[2, r], 16 + core)

    def four_back(i):
        r = zof(i)

        @pl.when(s >= 4)
        def _():
            wait_bytes(kv.at[3, r], kv_sem.at[2, r])

        if i not in DOWN:
            @pl.when((s >= 4) & (s + 4 < 32))
            def _():
                pass_on(kv.at[3, r], kv.at[4, r], f4_send, kv_sem.at[3, r], s + 4)

    def relayed(i):
        r = zof(i)
        n = DOWN.index(i)

        @pl.when(relays)
        def _():
            wait_bytes(relay.at[n], rl_sem.at[n])
            pass_on(relay.at[n], kv.at[4, r], mr_send, kv_sem.at[3, r], relay_dst)

    for j, dist in ((1, 1), (2, 2), (3, 4), (4, 8)):
        @pl.when(s < dist)
        def _():
            kv[j] = jnp.zeros(kv.shape[1:], BF16)
    for j in range(5):
        vx[j, :, D:] = jnp.ones((BLOCK, D), BF16)

    for step, i in PLAN:
        if step == "own":
            own(i)
        elif step == "two":
            two_back(i)
        elif step == "four":
            to_four(i)
        elif step == "relay":
            relayed(i)
        else:
            crossed(i)

    @pl.when(s >= 1)
    def _():
        @pl.loop(0, NZ)
        def _(i):
            wait_bytes(kv.at[1, i], kv_sem.at[0, i])

    for j in range(3):
        vx[j, :, :D] = kv[j, :, 1].reshape(BLOCK, D)

    flags = [(vis_ref[0, j] != 0) & (s >= 2 ** j) for j in range(4)]
    dims = (((1,), (1,)), ((), ()))

    def scores3(i, buf):
        q = qbuf[zof(i)].reshape(2 * RUN, D)
        for j in range(3):
            buf[:, j * BLOCK:(j + 1) * BLOCK] = lax.dot_general(
                q, kv[j, :, 0].reshape(BLOCK, D), dims, preferred_element_type=F32)

    row = lax.broadcasted_iota(jnp.int32, (2 * RUN, BLOCK), 0) % RUN
    column = lax.broadcasted_iota(jnp.int32, (2 * RUN, BLOCK), 1)
    ahead = column - row

    def soft3(i, buf, out):
        r = zof(i)
        s0 = jnp.where(ahead <= r * RUN, buf[:, :BLOCK], -HIDE)
        s1, s2 = buf[:, BLOCK:2 * BLOCK], buf[:, 2 * BLOCK:]
        top = jnp.max(s0, axis=1, keepdims=True)
        for part, flag in ((s1, flags[0]), (s2, flags[1])):
            here = jnp.max(part, axis=1, keepdims=True)
            top = jnp.where(flag, jnp.maximum(top, here), top)
        low = top * SCALE2
        peak[r] = jnp.broadcast_to(low, (2 * RUN, D))
        out[:, :BLOCK] = jnp.exp2(s0 * SCALE2 - low).astype(BF16)
        for n, (part, flag) in enumerate(((s1, flags[0]), (s2, flags[1]))):
            out[:, (n + 1) * BLOCK:(n + 2) * BLOCK] = jnp.exp2(
                part * SCALE2 - jnp.where(flag, low, HIDE)).astype(BF16)

    def value3(i, out):
        acc[zof(i)] = jnp.dot(out[...], vx[0:3].reshape(3 * BLOCK, 2 * D), preferred_element_type=F32)

    def query(i):
        r = zof(i)
        wait_bytes(qbuf.at[r], q_sem.at[r])

        @pl.when(i + AHEAD < NZ)
        def _():
            spread(i + AHEAD, q_pieces)

    def events(at):
        for step, k in LATER[at]:
            {"relay": relayed, "cross": crossed, "old": four_back}[step](k)

    query(0)
    scores3(0, s_a)
    query(1)
    scores3(1, s_b)
    soft3(0, s_a, p_a)

    @pl.loop(0, 3)
    def _(n):
        i = 2 * n
        for at in range(3):
            @pl.when(n == at)
            def _():
                events(2 * at)
        query(i + 2)
        value3(i, p_a)
        scores3(i + 2, s_a)
        soft3(i + 1, s_b, p_b)
        for at in range(3):
            @pl.when(n == at)
            def _():
                events(2 * at + 1)
        query(i + 3)
        value3(i + 1, p_b)
        scores3(i + 3, s_b)
        soft3(i + 2, s_a, p_a)

    value3(6, p_a)
    soft3(7, s_b, p_b)
    value3(7, p_b)
    events(6)
    def scores1(j, i, buf):
        buf[:, :BLOCK] = lax.dot_general(
            qbuf[zof(i)].reshape(2 * RUN, D), kv[j, :, 0].reshape(BLOCK, D), dims, preferred_element_type=F32)

    def soft1(j, i, buf, out):
        r = zof(i)
        flag = flags[j - 1]
        part = buf[:, :BLOCK]
        old = peak[r, :, 0:1]
        low = jnp.where(flag, jnp.maximum(old, jnp.max(part, axis=1, keepdims=True) * SCALE2), old)
        peak[r] = jnp.broadcast_to(low, (2 * RUN, D))
        acc[r] = acc[r] * jnp.exp2(old - low)
        out[:, :BLOCK] = jnp.exp2(part * SCALE2 - jnp.where(flag, low, HIDE)).astype(BF16)

    def value1(j, i, out):
        r = zof(i)
        total = acc[r] + jnp.dot(out[:, :BLOCK], vx[j], preferred_element_type=F32)
        if j < 4:
            acc[r] = total
            return
        done = (total[:, :D] / total[:, D:]).astype(BF16)
        obuf[r, :, :D] = done[:RUN]
        obuf[r, :, D:] = done[RUN:]
        for x in range(2):
            p = r * 2 + x
            src, dst = obuf.at[r, x * 64:(x + 1) * 64], o_ref.at[:, cols(h, 2 * D)]

            @pl.when(p == h)
            def _():
                pltpu.make_async_copy(src, dst, o_sem).start()

            @pl.when(p != h)
            def _():
                pltpu.make_async_remote_copy(src, dst, o_send, o_sem, device_id={"head": p}, device_id_type=MESH).start()

    def block(j):
        vx[j, :, :D] = kv[j, :, 1].reshape(BLOCK, D)
        scores1(j, 7, s_a)
        scores1(j, 6, s_b)
        soft1(j, 7, s_a, p_a)

        @pl.loop(0, 3)
        def _(n):
            i = 7 - 2 * n
            value1(j, i, p_a)
            scores1(j, i - 2, s_a)
            soft1(j, i - 1, s_b, p_b)
            value1(j, i - 1, p_b)
            scores1(j, i - 3, s_b)
            soft1(j, i - 2, s_a, p_a)

        value1(j, 1, p_a)
        soft1(j, 0, s_b, p_b)
        value1(j, 0, p_b)

    block(3)

    @pl.when(s >= 8)
    def _():
        @pl.loop(0, NZ)
        def _(i):
            wait_bytes(kv.at[4, i], kv_sem.at[3, i])

    block(4)

    wait_bytes(k_ref.at[:, :15 * D], in_send.at[0])
    wait_bytes(v_ref.at[:, :15 * D], in_send.at[1])
    wait_bytes(q_ref.at[:, :30 * D], in_send.at[2])
    whole = kv.at[0]
    for cond, ref, sem in (
        ((core == 0) | (s >= 2), whole, f1_send),
        (s + 2 < 32, whole, f2_send),
        ((s >= 2) & (s + 2 < 32), whole, f3_send),
        ((s >= 4) & (s + 4 < 32), kv.at[0, 0:NZ - NM], f4_send),
        (s + 8 < 32, kv.at[0, 0:NM], m_send),
        (relays, kv.at[0, 0:NM], mr_send),
        (is_cross, whole, cross_send),
    ):
        @pl.when(cond)
        def _():
            wait_bytes(ref, sem)
    wait_bytes(o_ref.at[:, :30 * D], o_send)
    wait_bytes(o_ref, o_sem)


def body(queries, keys, values, visible):
    dma = pltpu.SemaphoreType.DMA
    return pl.pallas_call(
        kernel,
        out_shape=pltpu.VMEM(queries.shape, BF16),
        in_specs=[pl.BlockSpec(memory_space=pltpu.SMEM)] + [pl.BlockSpec(memory_space=pl.ANY)] * 3,
        out_specs=pl.BlockSpec(memory_space=pltpu.VMEM),
        scratch_shapes=[
            pltpu.VMEM((NZ, 2, RUN, D), BF16),
            pltpu.VMEM((5, NZ, 2, RUN, D), BF16),
            pltpu.VMEM((NM, 2, RUN, D), BF16),
            pltpu.VMEM((NZ, 2, RUN, D), BF16),
            pltpu.VMEM((5, BLOCK, 2 * D), BF16),
            pltpu.VMEM((NZ, RUN, 2 * D), BF16),
            pltpu.VMEM((NZ, 2 * RUN, 2 * D), F32),
            pltpu.VMEM((NZ, 2 * RUN, D), F32),
            pltpu.VMEM((2 * RUN, 3 * BLOCK), F32),
            pltpu.VMEM((2 * RUN, 3 * BLOCK), F32),
            pltpu.VMEM((2 * RUN, 3 * BLOCK), BF16),
            pltpu.VMEM((2 * RUN, 3 * BLOCK), BF16),
            dma((NZ,)), dma((NZ,)), dma((4, NZ)), dma((NM,)), dma((NZ,)), dma,
            dma((3,)), dma, dma, dma, dma, dma, dma, dma, dma,
        ],
        compiler_params=pltpu.CompilerParams(
            collective_id=0, has_side_effects=True, vmem_limit_bytes=56 * 2**20),
        cost_estimate=pl.CostEstimate(flops=5 * 10**9, bytes_accessed=2 * 10**6, transcendentals=10**7),
    )(visible, queries, keys, values)


def solution(mesh):
    rows = P(("seq", "head"), None)
    return jax.shard_map(
        body,
        mesh=mesh,
        in_specs=(rows, rows, rows, P("seq", None)),
        out_specs=rows,
        check_vma=False,
    )
```

```python
import functools

import jax
import jax.numpy as jnp
from jax import lax
from jax.experimental import pallas as pl
from jax.experimental.pallas import tpu as pltpu
from jax.sharding import PartitionSpec as P

D = 128
RUN = 128
NZ = 8
BLOCK = 1024
SCALE2 = 168.0 ** (-0.5) * 1.4426950408889634
AHEAD = 8
DOWN = (0, 1, 5, 6, 7)
NM = len(DOWN)
HIDE = 1e30
PLAN = (
    ("own", 0),
    ("own", 1),
    ("own", 2),
    ("two", 0),
    ("relay", 0),
    ("own", 3),
    ("own", 4),
    ("two", 1),
    ("relay", 1),
    ("two", 2),
    ("own", 5),
    ("two", 3),
    ("own", 6),
    ("two", 4),
    ("own", 7),
    ("four", 0),
    ("four", 1),
    ("four", 2),
    ("four", 3),
    ("four", 4),
    ("two", 5),
    ("four", 5),
    ("cross", 0),
    ("two", 6),
    ("four", 6),
    ("relay", 5),
    ("cross", 1),
    ("two", 7),
    ("four", 7),
    ("cross", 2),
)
LATER = (
    (("cross", 3), ("old", 0), ),
    (("cross", 4), ("old", 1), ("relay", 6), ),
    (("cross", 5), ("old", 2), ),
    (("cross", 6), ("old", 3), ("relay", 7), ),
    (("cross", 7), ("old", 4), ),
    (("old", 5), ),
    (("old", 6), ("old", 7), ),
)
MESH = pl.DeviceIdType.MESH
F32 = jnp.float32
BF16 = jnp.bfloat16


def offset(i):
    return jnp.where(i % 2 == 1, (i + 1) // 2, (NZ - i // 2) % NZ)


def kernel(vis_ref, q_ref, k_ref, v_ref, o_ref, qbuf, kv, relay, cross, vx, obuf, acc, peak,
           s_a, s_b, p_a, p_b,
           kv0_sem, q_sem, kv_sem, rl_sem, cross_sem, o_sem, in_send, f1_send, f2_send, f3_send, f4_send,
           m_send, mr_send, cross_send, o_send):
    s = lax.axis_index("seq")
    h = lax.axis_index("head")
    z, xh = h // 2, h % 2
    core, chip = s % 2, s // 2
    xl, y = chip // 8, chip % 8

    def relay_of(c):
        return jnp.where((c >= 4) & (c < 8), c + 6, (c // 8) * 8 + (c % 8 + 6) % 8)

    relay_to = relay_of(chip) * 2 + core
    relays = (xl == 1) | (y >= 6) | (y <= 1)
    relay_from = jnp.where((y >= 2) & (y <= 5), y + 2, xl * 8 + (y + 2) % 8) * 2 + core
    relay_dst = relay_from + 8
    relay_src = relay_of(chip - 4) * 2 + core
    sends_cross, is_cross, gets_cross = chip == 7, chip == 15, chip == 8

    bar = pltpu.get_barrier_semaphore()

    @pl.loop(1, 16)
    def _(n):
        pl.semaphore_signal(bar, inc=1, device_id={"head": (h + n) % 16}, device_id_type=MESH)

    links = [
        (True, s + 1 - 2 * core),
        (s + 2 < 32, s + 2), (s >= 2, s - 2),
        (s + 4 < 32, s + 4), (s >= 4, s - 4),
        (s + 8 < 32, relay_to), (relays, relay_from),
        (relays, relay_dst), (s >= 8, relay_src),
        (sends_cross, 30 + core), (is_cross, 14 + core), (is_cross, 16 + core), (gets_cross, 30 + core),
    ]
    count = 15
    for cond, other in links:
        if cond is True:
            pl.semaphore_signal(bar, inc=1, device_id={"seq": other}, device_id_type=MESH)
            count = count + 1
        else:
            @pl.when(cond)
            def _():
                pl.semaphore_signal(bar, inc=1, device_id={"seq": other}, device_id_type=MESH)
            count = count + cond.astype(jnp.int32)
    pl.semaphore_wait(bar, count)

    def rows64(x):
        return pl.ds(pl.multiple_of(x * 64, 64), 64)

    def cols(i, width):
        return pl.ds(pl.multiple_of(i * width, width), width)

    def pieces(p):
        yield k_ref.at[:, cols(p, D)], kv.at[0, z, 0, rows64(xh)], in_send.at[0], kv0_sem.at[z]
        yield v_ref.at[:, cols(p, D)], kv.at[0, z, 1, rows64(xh)], in_send.at[1], kv0_sem.at[z]

    def q_pieces(p):
        for g in range(2):
            yield q_ref.at[:, cols(p * 2 + g, D)], qbuf.at[z, g, rows64(xh)], in_send.at[2], q_sem.at[z]

    for src, dst, _, sem in pieces(h):
        pltpu.make_async_copy(src, dst, sem).start()
    for src, dst, _, sem in q_pieces(h):
        pltpu.make_async_copy(src, dst, sem).start()

    def spread(i, each):
        for n in range(2):
            p = ((z + offset(i)) % NZ) * 2 + (xh + n) % 2

            @pl.when(p != h)
            def _():
                for src, dst, send, recv in each(p):
                    pltpu.make_async_remote_copy(
                        src, dst, send, recv, device_id={"head": p}, device_id_type=MESH).start()

    for i in range(AHEAD):
        spread(i, pieces)

    def zof(i):
        return (z + offset(i)) % NZ

    def wait_bytes(ref, sem):
        pltpu.make_async_copy(ref, ref, sem).wait()

    def pass_on(src, dst, send, recv, to):
        pltpu.make_async_remote_copy(src, dst, send, recv, device_id={"seq": to}, device_id_type=MESH).start()

    def own(i):
        r = zof(i)
        wait_bytes(kv.at[0, r], kv0_sem.at[r])
        if i + AHEAD < NZ:
            spread(i + AHEAD, pieces)
        else:
            spread(i + AHEAD - NZ, q_pieces)

        @pl.when(core == 0)
        def _():
            pass_on(kv.at[0, r], kv.at[1, r], f1_send, kv_sem.at[0, r], s + 1)

        @pl.when(s + 2 < 32)
        def _():
            pass_on(kv.at[0, r], kv.at[2, r], f2_send, kv_sem.at[1, r], s + 2)

        if i in DOWN:
            n = DOWN.index(i)

            @pl.when(s + 8 < 32)
            def _():
                pass_on(kv.at[0, r], relay.at[n], m_send, rl_sem.at[n], relay_to)

    def two_back(i):
        r = zof(i)

        @pl.when(s >= 2)
        def _():
            wait_bytes(kv.at[2, r], kv_sem.at[1, r])

        @pl.when((s >= 2) & (core == 1))
        def _():
            pass_on(kv.at[2, r], kv.at[1, r], f1_send, kv_sem.at[0, r], s - 1)

    def to_four(i):
        r = zof(i)

        @pl.when((s >= 2) & (s + 2 < 32) & (chip != 7))
        def _():
            pass_on(kv.at[2, r], kv.at[3, r], f3_send, kv_sem.at[2, r], s + 2)

        @pl.when(sends_cross)
        def _():
            pass_on(kv.at[2, r], cross.at[r], f3_send, cross_sem.at[r], 30 + core)

    def crossed(i):
        r = zof(i)

        @pl.when(is_cross)
        def _():
            wait_bytes(cross.at[r], cross_sem.at[r])
            pass_on(cross.at[r], kv.at[3, r], cross_send, kv_sem.at[2, r], 16 + core)

    def four_back(i):
        r = zof(i)

        @pl.when(s >= 4)
        def _():
            wait_bytes(kv.at[3, r], kv_sem.at[2, r])

        if i not in DOWN:
            @pl.when((s >= 4) & (s + 4 < 32))
            def _():
                pass_on(kv.at[3, r], kv.at[4, r], f4_send, kv_sem.at[3, r], s + 4)

    def relayed(i):
        r = zof(i)
        n = DOWN.index(i)

        @pl.when(relays)
        def _():
            wait_bytes(relay.at[n], rl_sem.at[n])
            pass_on(relay.at[n], kv.at[4, r], mr_send, kv_sem.at[3, r], relay_dst)

    for j, dist in ((1, 1), (2, 2), (3, 4), (4, 8)):
        @pl.when(s < dist)
        def _():
            kv[j] = jnp.zeros(kv.shape[1:], BF16)
    for j in range(5):
        vx[j, :, D:] = jnp.ones((BLOCK, D), BF16)

    for step, i in PLAN:
        if step == "own":
            own(i)
        elif step == "two":
            two_back(i)
        elif step == "four":
            to_four(i)
        elif step == "relay":
            relayed(i)
        else:
            crossed(i)

    @pl.when(s >= 1)
    def _():
        @pl.loop(0, NZ)
        def _(i):
            wait_bytes(kv.at[1, i], kv_sem.at[0, i])

    for j in range(3):
        vx[j, :, :D] = kv[j, :, 1].reshape(BLOCK, D)

    flags = [(vis_ref[0, j] != 0) & (s >= 2 ** j) for j in range(4)]
    dims = (((1,), (1,)), ((), ()))

    def scores3(i, buf):
        q = qbuf[zof(i)].reshape(2 * RUN, D)
        for j in range(3):
            buf[:, j * BLOCK:(j + 1) * BLOCK] = lax.dot_general(
                q, kv[j, :, 0].reshape(BLOCK, D), dims, preferred_element_type=F32)

    row = lax.broadcasted_iota(jnp.int32, (2 * RUN, BLOCK), 0) % RUN
    column = lax.broadcasted_iota(jnp.int32, (2 * RUN, BLOCK), 1)
    ahead = column - row

    def soft3(i, buf, out):
        r = zof(i)
        s0 = jnp.where(ahead <= r * RUN, buf[:, :BLOCK], -HIDE)
        s1, s2 = buf[:, BLOCK:2 * BLOCK], buf[:, 2 * BLOCK:]
        top = jnp.max(s0, axis=1, keepdims=True)
        for part, flag in ((s1, flags[0]), (s2, flags[1])):
            here = jnp.max(part, axis=1, keepdims=True)
            top = jnp.where(flag, jnp.maximum(top, here), top)
        low = top * SCALE2
        peak[r] = jnp.broadcast_to(low, (2 * RUN, D))
        out[:, :BLOCK] = jnp.exp2(s0 * SCALE2 - low).astype(BF16)
        for n, (part, flag) in enumerate(((s1, flags[0]), (s2, flags[1]))):
            out[:, (n + 1) * BLOCK:(n + 2) * BLOCK] = jnp.exp2(
                part * SCALE2 - jnp.where(flag, low, HIDE)).astype(BF16)

    def value3(i, out):
        acc[zof(i)] = jnp.dot(out[...], vx[0:3].reshape(3 * BLOCK, 2 * D), preferred_element_type=F32)

    def query(i):
        r = zof(i)
        wait_bytes(qbuf.at[r], q_sem.at[r])

        @pl.when(i + AHEAD < NZ)
        def _():
            spread(i + AHEAD, q_pieces)

    def events(at):
        for step, k in LATER[at]:
            {"relay": relayed, "cross": crossed, "old": four_back}[step](k)

    query(0)
    scores3(0, s_a)
    query(1)
    scores3(1, s_b)
    soft3(0, s_a, p_a)

    @pl.loop(0, 3)
    def _(n):
        i = 2 * n
        for at in range(3):
            @pl.when(n == at)
            def _():
                events(2 * at)
        query(i + 2)
        value3(i, p_a)
        scores3(i + 2, s_a)
        soft3(i + 1, s_b, p_b)
        for at in range(3):
            @pl.when(n == at)
            def _():
                events(2 * at + 1)
        query(i + 3)
        value3(i + 1, p_b)
        scores3(i + 3, s_b)
        soft3(i + 2, s_a, p_a)

    value3(6, p_a)
    soft3(7, s_b, p_b)
    value3(7, p_b)
    events(6)
    def scores1(j, i, buf):
        buf[:, :BLOCK] = lax.dot_general(
            qbuf[zof(i)].reshape(2 * RUN, D), kv[j, :, 0].reshape(BLOCK, D), dims, preferred_element_type=F32)

    def soft1(j, i, buf, out):
        r = zof(i)
        flag = flags[j - 1]
        part = buf[:, :BLOCK]
        old = peak[r, :, 0:1]
        low = jnp.where(flag, jnp.maximum(old, jnp.max(part, axis=1, keepdims=True) * SCALE2), old)
        peak[r] = jnp.broadcast_to(low, (2 * RUN, D))
        acc[r] = acc[r] * jnp.exp2(old - low)
        out[:, :BLOCK] = jnp.exp2(part * SCALE2 - jnp.where(flag, low, HIDE)).astype(BF16)

    def value1(j, i, out):
        r = zof(i)
        total = acc[r] + jnp.dot(out[:, :BLOCK], vx[j], preferred_element_type=F32)
        if j < 4:
            acc[r] = total
            return
        done = (total[:, :D] / total[:, D:]).astype(BF16)
        obuf[r, :, :D] = done[:RUN]
        obuf[r, :, D:] = done[RUN:]
        for x in range(2):
            p = r * 2 + x
            src, dst = obuf.at[r, x * 64:(x + 1) * 64], o_ref.at[:, cols(h, 2 * D)]

            @pl.when(p == h)
            def _():
                pltpu.make_async_copy(src, dst, o_sem).start()

            @pl.when(p != h)
            def _():
                pltpu.make_async_remote_copy(src, dst, o_send, o_sem, device_id={"head": p}, device_id_type=MESH).start()

    def block(j):
        vx[j, :, :D] = kv[j, :, 1].reshape(BLOCK, D)
        scores1(j, 7, s_a)
        scores1(j, 6, s_b)
        soft1(j, 7, s_a, p_a)

        @pl.loop(0, 3)
        def _(n):
            i = 7 - 2 * n
            value1(j, i, p_a)
            scores1(j, i - 2, s_a)
            soft1(j, i - 1, s_b, p_b)
            value1(j, i - 1, p_b)
            scores1(j, i - 3, s_b)
            soft1(j, i - 2, s_a, p_a)

        value1(j, 1, p_a)
        soft1(j, 0, s_b, p_b)
        value1(j, 0, p_b)

    block(3)

    @pl.when(s >= 8)
    def _():
        @pl.loop(0, NZ)
        def _(i):
            wait_bytes(kv.at[4, i], kv_sem.at[3, i])

    block(4)

    wait_bytes(k_ref.at[:, :15 * D], in_send.at[0])
    wait_bytes(v_ref.at[:, :15 * D], in_send.at[1])
    wait_bytes(q_ref.at[:, :30 * D], in_send.at[2])
    whole = kv.at[0]
    for cond, ref, sem in (
        ((core == 0) | (s >= 2), whole, f1_send),
        (s + 2 < 32, whole, f2_send),
        ((s >= 2) & (s + 2 < 32), whole, f3_send),
        ((s >= 4) & (s + 4 < 32), kv.at[0, 0:NZ - NM], f4_send),
        (s + 8 < 32, kv.at[0, 0:NM], m_send),
        (relays, kv.at[0, 0:NM], mr_send),
        (is_cross, whole, cross_send),
    ):
        @pl.when(cond)
        def _():
            wait_bytes(ref, sem)
    wait_bytes(o_ref.at[:, :30 * D], o_send)
    wait_bytes(o_ref, o_sem)


def body(queries, keys, values, visible):
    dma = pltpu.SemaphoreType.DMA
    return pl.pallas_call(
        kernel,
        out_shape=pltpu.VMEM(queries.shape, BF16),
        in_specs=[pl.BlockSpec(memory_space=pltpu.SMEM)] + [pl.BlockSpec(memory_space=pl.ANY)] * 3,
        out_specs=pl.BlockSpec(memory_space=pltpu.VMEM),
        scratch_shapes=[
            pltpu.VMEM((NZ, 2, RUN, D), BF16),
            pltpu.VMEM((5, NZ, 2, RUN, D), BF16),
            pltpu.VMEM((NM, 2, RUN, D), BF16),
            pltpu.VMEM((NZ, 2, RUN, D), BF16),
            pltpu.VMEM((5, BLOCK, 2 * D), BF16),
            pltpu.VMEM((NZ, RUN, 2 * D), BF16),
            pltpu.VMEM((NZ, 2 * RUN, 2 * D), F32),
            pltpu.VMEM((NZ, 2 * RUN, D), F32),
            pltpu.VMEM((2 * RUN, 3 * BLOCK), F32),
            pltpu.VMEM((2 * RUN, 3 * BLOCK), F32),
            pltpu.VMEM((2 * RUN, 3 * BLOCK), BF16),
            pltpu.VMEM((2 * RUN, 3 * BLOCK), BF16),
            dma((NZ,)), dma((NZ,)), dma((4, NZ)), dma((NM,)), dma((NZ,)), dma,
            dma((3,)), dma, dma, dma, dma, dma, dma, dma, dma,
        ],
        compiler_params=pltpu.CompilerParams(
            collective_id=0, has_side_effects=True, vmem_limit_bytes=56 * 2**20),
        cost_estimate=pl.CostEstimate(flops=5 * 10**9, bytes_accessed=2 * 10**6, transcendentals=10**7),
    )(visible, queries, keys, values)


def solution(mesh):
    rows = P(("seq", "head"), None)
    return jax.shard_map(
        body,
        mesh=mesh,
        in_specs=(rows, rows, rows, P("seq", None)),
        out_specs=rows,
        check_vma=False,
    )
```
